32 devices in a mesh: groups: 2 (over y), row: 4 (over x, core), col: 4 (over z).
Axes of the slice: x: 2, y: 2, z: 4, core: 2. Of those that a mesh axis runs over, the one named last changes fastest.
Arguments:
- pair_act: bfloat16 [320, 160, 128], P(('groups', 'row'), 'col'), parts along dimension 0, may hold values from -6 to 6
- lengths: int32 [8], P('groups'), parts along dimension 0, may hold values from 10 to 40, as said below
- in_gain: float32 [128], replicated, may hold values from 0.5 to 1.5
- in_bias: float32 [128], replicated, may hold values from -3 to 3
- w_left: bfloat16 [128, 256], replicated, may hold values from -0.5 to 0.5
- w_right: bfloat16 [128, 256], replicated, may hold values from -0.5 to 0.5
- w_gate: bfloat16 [128, 128], replicated, may hold values from -0.5 to 0.5
- mid_gain: float32 [128], replicated, may hold values from 0.5 to 1.5
- mid_bias: float32 [128], replicated, may hold values from -3 to 3
- w_out: bfloat16 [128, 128], replicated, may hold values from -0.5 to 0.5
Outputs:
- update: bfloat16 [320, 160, 128], P(('groups', 'row'), 'col'), parts along dimension 0
The draws below stay inside these ranges and needn't reach their ends.
There are 2 independent parts, one for each index of `groups`. The reference program is written for one: setup_inputs(seed, part) draws one part's arguments, and reference() takes and returns one part's arrays. A program takes and returns all parts, laid end to end along the dimension named above; an argument that names none is the same for every part. Nothing has to cross between parts.
Inputs may be any that keep to these rules, and one draw needn't show every extreme that they name: lengths of chains; some chain fills all 40 positions.
All inputs are finite; a program needn't handle non-finite values.
Results may differ from the reference program's by a relative error of at most 0.0057.
Values may be sent and summed in bfloat16 or wider, within the bound.
A program may use at most 128 MiB of HBM per device.

```python
import jax
import jax.numpy as jnp
from jax import lax

C = 128
CH = 128
CHAINS = 4
N = 160
SLOT = 40


def draw_lengths(key, part):
    key = jax.random.fold_in(key, 1)
    first_key, second_key = jax.random.split(key)
    raw_lengths = jax.random.randint(first_key, (CHAINS,), SLOT // 4, SLOT + 1)
    full_chain = jax.random.randint(second_key, (), 0, CHAINS)
    chain_ids = jnp.arange(CHAINS, dtype=jnp.int32)
    return jnp.where(chain_ids == full_chain, SLOT, raw_lengths).astype(jnp.int32)


def levels(own_key, extent, cuts, smallest, largest):
    factor_of = 1.0
    for position, shards_of in cuts:
        heights = jax.random.uniform(jax.random.fold_in(jax.random.fold_in(own_key, 6), position), (shards_of,), jnp.float32, smallest / len(cuts), largest / len(cuts))
        factor_of = factor_of * jnp.repeat(jnp.exp(heights), extent[position] // shards_of).reshape((-1,) + (1,) * (len(extent) - 1 - position))
    return factor_of


def normal_values(key, extent, deviation, bound, pieces=(), held_as=jnp.bfloat16):
    result = jax.random.normal(key, extent, jnp.float32) * deviation
    if len(pieces) > 0:
        result = levels(key, extent, pieces, -0.22, 0.18) * result
    return jnp.clip(result, min=-bound, max=bound).astype(held_as)


def setup_inputs(seed: int = 0, part: int = 0) -> dict:
    key_of = jax.random.split(jax.random.key(seed), 11)
    part_splits = jax.random.split(jax.random.fold_in(key_of[10], part), 11)
    pair_act = normal_values(part_splits[0], (N, N, C), 1.0, 6.0, ((0, 4), (1, 4)))
    lengths = draw_lengths(jax.random.fold_in(jax.random.fold_in(key_of[10], part), 71), part)
    in_gain = jnp.clip(1.0 + 0.1 * jax.random.normal(key_of[2], (C,), jnp.float32), 0.5, 1.5)
    in_bias = normal_values(key_of[3], (C,), 0.5, 3.0, (), jnp.float32)
    w_left = normal_values(key_of[4], (C, 2 * CH), C ** -0.5, 0.5)
    w_right = normal_values(key_of[5], (C, 2 * CH), C ** -0.5, 0.5)
    w_gate = normal_values(key_of[6], (C, C), C ** -0.5, 0.5)
    mid_gain = jnp.clip(1.0 + 0.1 * jax.random.normal(key_of[7], (CH,), jnp.float32), 0.5, 1.5)
    mid_bias = normal_values(key_of[8], (CH,), 0.5, 3.0, (), jnp.float32)
    w_out = normal_values(key_of[9], (CH, C), CH ** -0.5, 0.5)
    return {"pair_act": pair_act, "lengths": lengths, "in_gain": in_gain, "in_bias": in_bias, "w_left": w_left, "w_right": w_right, "w_gate": w_gate, "mid_gain": mid_gain, "mid_bias": mid_bias, "w_out": w_out}


def layer_norm(values, gain, bias):
    center = lax.optimization_barrier(jnp.mean(values, axis=-1, keepdims=True))
    spread = lax.optimization_barrier(jnp.mean(jnp.square(values - center), axis=-1, keepdims=True))
    return (values - center) / jnp.sqrt(spread + 1e-05) * gain + bias

def reference(pair_act, lengths, in_gain, in_bias, w_left, w_right, w_gate, mid_gain, mid_bias, w_out):
    pair_norm = layer_norm(pair_act.astype(jnp.float32), in_gain, in_bias).astype(jnp.bfloat16)
    residue_ids = jnp.arange(N, dtype=jnp.int32)
    chain_of = (residue_ids // SLOT).astype(jnp.int32)
    present = (residue_ids % SLOT < lengths[chain_of]).astype(jnp.float32)
    pair_mask = present[:, None] * present[None, :]
    flat = pair_norm.reshape(N * N, C)

    def edge_panel(weight):
        projected = jnp.dot(flat, weight, preferred_element_type=jnp.float32).reshape(N, N, 2 * CH)
        gated = pair_mask[:, :, None] * jax.nn.sigmoid(projected[:, :, CH:]) * projected[:, :, :CH]
        return gated.astype(jnp.bfloat16)
    left_edge = edge_panel(w_left)
    right_edge = edge_panel(w_right)
    triangle = jnp.einsum('ikh,jkh->ijh', left_edge.astype(jnp.float32), right_edge.astype(jnp.float32))
    normed = layer_norm(triangle, mid_gain, mid_bias).astype(jnp.bfloat16)
    out_gate = jax.nn.sigmoid(jnp.dot(flat, w_gate, preferred_element_type=jnp.float32))
    projected_out = jnp.dot(normed.reshape(N * N, CH), w_out, preferred_element_type=jnp.float32)
    return (out_gate * projected_out).reshape(N, N, C).astype(jnp.bfloat16)
```

```python
import functools

import jax
import jax.numpy as jnp
from jax import lax
from jax.experimental import pallas as pl
from jax.experimental.pallas import tpu as pltpu
from jax.sharding import PartitionSpec as P


def layer_norm(values, gain, bias):
    center = jnp.mean(values, axis=-1, keepdims=True)
    spread = jnp.mean(jnp.square(values - center), axis=-1, keepdims=True)
    return (values - center) / jnp.sqrt(spread + 1e-05) * gain + bias


def in_crop(residue_ids, lengths, slot_len):
    chain_of = residue_ids // slot_len
    chosen = chain_of[:, None] == jnp.arange(lengths.shape[0], dtype=jnp.int32)[None, :]
    chain_len = jnp.sum(jnp.where(chosen, lengths[None, :], 0), axis=1)
    return (residue_ids % slot_len < chain_len).astype(jnp.float32)


def plain_shards(pair_act, lengths, in_gain, in_bias, w_left, w_right, w_gate, mid_gain, mid_bias, w_out):
    rows_here, cols_here, width = pair_act.shape
    hidden = w_out.shape[0]
    residues = rows_here * lax.axis_size("row")
    slot_len = residues // lengths.shape[0]
    row_ids = lax.axis_index("row") * rows_here + jnp.arange(rows_here, dtype=jnp.int32)
    col_ids = lax.axis_index("col") * cols_here + jnp.arange(cols_here, dtype=jnp.int32)
    pair_mask = (
        in_crop(row_ids, lengths, slot_len)[:, None] * in_crop(col_ids, lengths, slot_len)[None, :]
    )
    pair_norm = layer_norm(pair_act.astype(jnp.float32), in_gain, in_bias).astype(jnp.bfloat16)
    pair_norm = pair_norm.reshape(rows_here * cols_here, width)

    def edge_panel(weight):
        projected = jnp.dot(pair_norm, weight, preferred_element_type=jnp.float32)
        projected = projected.reshape(rows_here, cols_here, 2 * hidden)
        gated = (
            pair_mask[:, :, None]
            * jax.nn.sigmoid(projected[:, :, hidden:])
            * projected[:, :, :hidden]
        )
        return jnp.transpose(gated.astype(jnp.bfloat16), (2, 0, 1))

    left_edge = edge_panel(w_left)
    right_edge = edge_panel(w_right)
    partial_value = jnp.einsum(
        "hik,hjk->hij",
        left_edge,
        lax.all_gather(right_edge, "row", axis=1, tiled=True),
        preferred_element_type=jnp.float32,
    )
    triangle = lax.psum_scatter(partial_value, "col", scatter_dimension=2, tiled=True)
    triangle = jnp.transpose(triangle, (1, 2, 0))
    normed = layer_norm(triangle, mid_gain, mid_bias).astype(jnp.bfloat16)
    out_gate = jax.nn.sigmoid(jnp.dot(pair_norm, w_gate, preferred_element_type=jnp.float32))
    projected_out = jnp.dot(
        normed.reshape(rows_here * cols_here, hidden), w_out, preferred_element_type=jnp.float32
    )
    return (out_gate * projected_out).reshape(rows_here, cols_here, width).astype(jnp.bfloat16)


MESH = pl.DeviceIdType.MESH
ROW, COL = 4, 4
CHUNKS = 4
PIECE = 4


def half_gate(values):
    return 0.5 * jnp.tanh(0.5 * values) + 0.5


def fused_kernel(
    lengths_ref, pair_ref, in_gain_ref, in_bias_ref, w_left_ref, w_right_ref, w_gate_ref,
    mid_gain_ref, mid_bias_ref, w_out_ref, out_ref,
    held, left_edge, right_edge, triangle, gate, got_sem, chain_sem, cross_sem,
    *, side, slot_len,
):
    group, r, c = lax.axis_index("groups"), lax.axis_index("row"), lax.axis_index("col")
    positions, width = pair_ref.shape
    chunk = positions // CHUNKS
    piece = PIECE * side
    pieces = positions // piece
    tiles = side // 8
    chains = lengths_ref.shape[0]
    is_source = r == c
    same_core = r % 2 == c % 2
    same_chip = r // 2 == c // 2
    relays = jnp.logical_and(same_core, jnp.logical_not(same_chip))
    sibling = r + 1 - 2 * (r % 2)
    across = (r + 2) % ROW

    def present(first, extent):
        ids = first + lax.broadcasted_iota(jnp.int32, extent, len(extent) - 2)
        chosen = jnp.zeros(extent, jnp.float32)
        for chain in range(chains):
            start = chain * slot_len
            inside = jnp.logical_and(ids >= start, ids < start + lengths_ref[chain])
            inside = jnp.logical_and(inside, ids < start + slot_len)
            chosen = chosen + jnp.where(inside, 1.0, 0.0)
        return chosen

    def rows_of(part):
        return pl.ds(pl.multiple_of(part * chunk, 16), chunk)

    def transfer(source, target, part, send, device):
        return pltpu.make_async_remote_copy(
            src_ref=held.at[source, rows_of(part), :],
            dst_ref=held.at[target, rows_of(part), :],
            send_sem=send,
            recv_sem=got_sem.at[target, part],
            device_id=device,
            device_id_type=MESH,
        )

    def chain_copy(k, part, way):
        return transfer(k, k, part, chain_sem.at[k, part, way], (group, r, c + 2 * way - 1))

    def cross_copy(source, k, part, way):
        target = sibling if way == 0 else across
        return transfer(source, COL + k, part, cross_sem.at[k, part, way], (group, target, c))

    def chain_sends(k, part, finish):
        for way in range(2):
            fits = jnp.logical_and(k >= c, c > 0) if way == 0 else jnp.logical_and(k <= c, c < COL - 1)

            @pl.when(fits)
            def _():
                copy = chain_copy(k, part, way)
                copy.wait_send() if finish else copy.start()

    def source_sends(k, part, finish):
        @pl.when(is_source)
        def _():
            for way in (1, 0):
                copy = cross_copy(k, k, part, way)
                copy.wait_send() if finish else copy.start()

    def relay_sends(k, part, finish):
        @pl.when(relays)
        def _():
            copy = cross_copy(COL + k, k, part, 0)
            copy.wait_send() if finish else copy.start()

    def normalise(values, gain_ref, bias_ref):
        center = jnp.mean(values, axis=-1, keepdims=True)
        moved = values - center
        spread = jnp.mean(jnp.square(moved), axis=-1, keepdims=True)
        return moved * lax.rsqrt(spread + 1e-05) * gain_ref[...] + bias_ref[...]

    barrier = pltpu.get_barrier_semaphore()
    for step in range(1, ROW):
        pl.semaphore_signal(
            barrier, inc=1, device_id=(group, (r + step) % ROW, c), device_id_type=MESH
        )

    @pl.when(c > 0)
    def _():
        pl.semaphore_signal(barrier, inc=1, device_id=(group, r, c - 1), device_id_type=MESH)

    @pl.when(c < COL - 1)
    def _():
        pl.semaphore_signal(barrier, inc=1, device_id=(group, r, c + 1), device_id_type=MESH)

    def norm_piece(part):
        rows = rows_of(part)
        values = pair_ref[rows, :].astype(jnp.float32)
        held[c, rows, :] = normalise(values, in_gain_ref, in_bias_ref).astype(jnp.bfloat16)

    norm_piece(0)
    pl.semaphore_wait(
        barrier, ROW - 1 + jnp.where(c > 0, 1, 0) + jnp.where(c < COL - 1, 1, 0)
    )
    for part in range(CHUNKS):
        if part > 0:
            norm_piece(part)
        chain_sends(c, part, False)
        source_sends(c, part, False)

    def piece_rows(t):
        return pl.ds(pl.multiple_of(t * piece, 16), piece)

    def own_piece(t, carry):
        rows = piece_rows(t)
        gate[rows, :] = half_gate(
            jnp.dot(held[c, rows, :], w_gate_ref[...], preferred_element_type=jnp.float32)
        )
        triangle[rows, :] = jnp.zeros((piece, width), jnp.float32)
        return carry

    lax.fori_loop(0, pieces, own_piece, 0)

    def edge(slot, weight_ref, rows):
        projected = jnp.dot(
            held[slot, rows, :], weight_ref[...], preferred_element_type=jnp.float32
        )
        return projected[:, :width] * half_gate(projected[:, width:])

    def left_part(k):
        def left_piece(t, carry):
            rows = piece_rows(t)
            left_edge[rows, :] = edge(k, w_left_ref, rows)
            return carry

        lax.fori_loop(0, pieces, left_piece, 0)

    def right_part(k):
        slot = jnp.where(is_source, k, COL + k)
        mask_k = present(k * side, (side, width))

        def right_piece(t, carry):
            rows = piece_rows(t)
            value = edge(slot, w_right_ref, rows).reshape(PIECE, side, width) * mask_k[None]
            right_edge[rows, :] = value.reshape(piece, width)
            return carry

        lax.fori_loop(0, pieces, right_piece, 0)

    def multiply():
        def some_rows(block, carry):
            base = pl.multiple_of(block * (8 * side), 8)

            def add_k(k, sums):
                rights = [
                    right_edge[pl.ds(tile * 8 * side + k, 8, stride=side), :]
                    for tile in range(tiles)
                ]
                new = []
                for i in range(8):
                    left = left_edge[pl.ds(base + i * side + k, 1), :]
                    for tile in range(tiles):
                        new.append(sums[i * tiles + tile] + left * rights[tile])
                return tuple(new)

            where = [
                pl.ds(pl.multiple_of(base + i * side + tile * 8, 8), 8)
                for i in range(8)
                for tile in range(tiles)
            ]
            sums = tuple(triangle[rows, :] for rows in where)
            sums = lax.fori_loop(0, side, add_k, sums, unroll=4)
            for rows, value in zip(where, sums):
                triangle[rows, :] = value
            return carry

        lax.fori_loop(0, side // 8, some_rows, 0)

    def at_distance(distance, act):
        for sign in (-1, 1) if distance > 0 else (1,):
            k = c + sign * distance

            @pl.when(jnp.logical_and(k >= 0, k < COL))
            def _():
                act(k)

    def gather(distance):
        def pass_on(part, carry):
            def act(k):
                chain_copy(k, part, 0).wait_recv()
                chain_sends(k, part, False)
                source_sends(k, part, False)

            at_distance(distance, act)
            return carry

        lax.fori_loop(0, CHUNKS, pass_on, 0)

    def receive_right(k):
        @pl.when(jnp.logical_not(is_source))
        def _():
            def pass_on(part, carry):
                cross_copy(k, k, part, 0).wait_recv()
                relay_sends(k, part, False)
                return carry

            lax.fori_loop(0, CHUNKS, pass_on, 0)

    def work(k):
        left_part(k)
        receive_right(k)
        right_part(k)
        multiply()

    for distance in range(1, COL):
        gather(distance)
        at_distance(distance - 1, work)
    at_distance(COL - 1, work)

    mask_j = present(c * side, (side, width))

    def finish_piece(t, carry):
        rows = piece_rows(t)
        parts = []
        for i in range(PIECE):
            mask_i = present(r * side + t * PIECE + i, (1, width))
            parts.append(mask_i * mask_j)
        mask = jnp.concatenate(parts, axis=0)
        normed = normalise(triangle[rows, :] * mask, mid_gain_ref, mid_bias_ref)
        projected = jnp.dot(
            normed.astype(jnp.bfloat16), w_out_ref[...], preferred_element_type=jnp.float32
        )
        out_ref[rows, :] = (gate[rows, :] * projected).astype(out_ref.dtype)
        return carry

    lax.fori_loop(0, pieces, finish_piece, 0)

    def drain(index, carry):
        k, part = index // CHUNKS, index % CHUNKS
        chain_sends(k, part, True)
        source_sends(k, part, True)
        relay_sends(k, part, True)
        return carry

    lax.fori_loop(0, COL * CHUNKS, drain, 0)


def fused_shards(pair_act, lengths, in_gain, in_bias, w_left, w_right, w_gate, mid_gain, mid_bias, w_out):
    side, _, width = pair_act.shape
    positions = side * side
    slot_len = side * ROW // lengths.shape[0]
    vmem = pl.BlockSpec(memory_space=pltpu.VMEM)
    out = pl.pallas_call(
        functools.partial(fused_kernel, side=side, slot_len=slot_len),
        out_shape=jax.ShapeDtypeStruct((positions, width), jnp.bfloat16),
        in_specs=[pl.BlockSpec(memory_space=pltpu.SMEM)] + [vmem] * 9,
        out_specs=vmem,
        scratch_shapes=[
            pltpu.VMEM((2 * COL, positions, width), jnp.bfloat16),
            pltpu.VMEM((positions, width), jnp.float32),
            pltpu.VMEM((positions, width), jnp.float32),
            pltpu.VMEM((positions, width), jnp.float32),
            pltpu.VMEM((positions, width), jnp.float32),
            pltpu.SemaphoreType.DMA((2 * COL, CHUNKS)),
            pltpu.SemaphoreType.DMA((COL, CHUNKS, 2)),
            pltpu.SemaphoreType.DMA((COL, CHUNKS, 2)),
        ],
        compiler_params=pltpu.CompilerParams(
            collective_id=0, has_side_effects=True, vmem_limit_bytes=32 * 1024 * 1024
        ),
    )(
        lengths, pair_act.reshape(positions, width), in_gain[None], in_bias[None], w_left, w_right,
        w_gate, mid_gain[None], mid_bias[None], w_out,
    )
    return out.reshape(side, side, width)


def solution(mesh):
    in_specs = (
        P(("groups", "row"), "col", None),
        P("groups"),
        P(),
        P(),
        P(),
        P(),
        P(),
        P(),
        P(),
        P(),
    )
    out_specs = P(("groups", "row"), "col", None)
    shards = plain_shards
    if mesh.shape["row"] == 4 and mesh.shape["col"] == 4:
        shards = fused_shards
    return jax.shard_map(shards, mesh=mesh, in_specs=in_specs, out_specs=out_specs, check_vma=False)
```

```python
import functools

import jax
import jax.numpy as jnp
from jax import lax
from jax.experimental import pallas as pl
from jax.experimental.pallas import tpu as pltpu
from jax.sharding import PartitionSpec as P


def layer_norm(values, gain, bias):
    center = jnp.mean(values, axis=-1, keepdims=True)
    spread = jnp.mean(jnp.square(values - center), axis=-1, keepdims=True)
    return (values - center) / jnp.sqrt(spread + 1e-05) * gain + bias


def in_crop(residue_ids, lengths, slot_len):
    chain_of = residue_ids // slot_len
    chosen = chain_of[:, None] == jnp.arange(lengths.shape[0], dtype=jnp.int32)[None, :]
    chain_len = jnp.sum(jnp.where(chosen, lengths[None, :], 0), axis=1)
    return (residue_ids % slot_len < chain_len).astype(jnp.float32)


def plain_shards(pair_act, lengths, in_gain, in_bias, w_left, w_right, w_gate, mid_gain, mid_bias, w_out):
    rows_here, cols_here, width = pair_act.shape
    hidden = w_out.shape[0]
    residues = rows_here * lax.axis_size("row")
    slot_len = residues // lengths.shape[0]
    row_ids = lax.axis_index("row") * rows_here + jnp.arange(rows_here, dtype=jnp.int32)
    col_ids = lax.axis_index("col") * cols_here + jnp.arange(cols_here, dtype=jnp.int32)
    pair_mask = (
        in_crop(row_ids, lengths, slot_len)[:, None] * in_crop(col_ids, lengths, slot_len)[None, :]
    )
    pair_norm = layer_norm(pair_act.astype(jnp.float32), in_gain, in_bias).astype(jnp.bfloat16)
    pair_norm = pair_norm.reshape(rows_here * cols_here, width)

    def edge_panel(weight):
        projected = jnp.dot(pair_norm, weight, preferred_element_type=jnp.float32)
        projected = projected.reshape(rows_here, cols_here, 2 * hidden)
        gated = (
            pair_mask[:, :, None]
            * jax.nn.sigmoid(projected[:, :, hidden:])
            * projected[:, :, :hidden]
        )
        return jnp.transpose(gated.astype(jnp.bfloat16), (2, 0, 1))

    left_edge = edge_panel(w_left)
    right_edge = edge_panel(w_right)
    partial_value = jnp.einsum(
        "hik,hjk->hij",
        left_edge,
        lax.all_gather(right_edge, "row", axis=1, tiled=True),
        preferred_element_type=jnp.float32,
    )
    triangle = lax.psum_scatter(partial_value, "col", scatter_dimension=2, tiled=True)
    triangle = jnp.transpose(triangle, (1, 2, 0))
    normed = layer_norm(triangle, mid_gain, mid_bias).astype(jnp.bfloat16)
    out_gate = jax.nn.sigmoid(jnp.dot(pair_norm, w_gate, preferred_element_type=jnp.float32))
    projected_out = jnp.dot(
        normed.reshape(rows_here * cols_here, hidden), w_out, preferred_element_type=jnp.float32
    )
    return (out_gate * projected_out).reshape(rows_here, cols_here, width).astype(jnp.bfloat16)


MESH = pl.DeviceIdType.MESH
ROW, COL = 4, 4
CHUNKS = 2
PIECE = 40


def half_gate(values):
    return 0.5 * jnp.tanh(0.5 * values) + 0.5


def fused_kernel(
    lengths_hbm, pair_hbm, in_gain_hbm, in_bias_hbm, w_left_hbm, w_right_hbm, w_gate_hbm,
    mid_gain_hbm, mid_bias_hbm, w_out_hbm, out_ref,
    lengths_ref, pair_ref, in_gain_ref, in_bias_ref, w_left_ref, w_right_ref, w_gate_ref,
    mid_gain_ref, mid_bias_ref, w_out_ref, load_sem, held, left_edge, right_edge, triangle, gate, got_sem, chain_sem, cross_sem,
    *, side, slot_len,
):
    group, r, c = lax.axis_index("groups"), lax.axis_index("row"), lax.axis_index("col")
    positions, width = pair_ref.shape
    chunk = positions // CHUNKS
    piece = PIECE * side
    pieces = positions // piece
    tiles = side // 8
    chains = lengths_ref.shape[0]
    is_source = r == c
    same_core = r % 2 == c % 2
    same_chip = r // 2 == c // 2
    relays = jnp.logical_and(same_core, jnp.logical_not(same_chip))
    sibling = r + 1 - 2 * (r % 2)
    across = (r + 2) % ROW

    def present(first, extent):
        ids = first + lax.broadcasted_iota(jnp.int32, extent, len(extent) - 2)
        chosen = jnp.zeros(extent, jnp.float32)
        for chain in range(chains):
            start = chain * slot_len
            inside = jnp.logical_and(ids >= start, ids < start + lengths_ref[chain])
            inside = jnp.logical_and(inside, ids < start + slot_len)
            chosen = chosen + jnp.where(inside, 1.0, 0.0)
        return chosen

    def rows_of(part):
        return pl.ds(pl.multiple_of(part * chunk, 16), chunk)

    def transfer(source, target, part, send, device):
        return pltpu.make_async_remote_copy(
            src_ref=held.at[source, rows_of(part), :],
            dst_ref=held.at[target, rows_of(part), :],
            send_sem=send,
            recv_sem=got_sem.at[target, part],
            device_id=device,
            device_id_type=MESH,
        )

    def chain_copy(k, part, way):
        return transfer(k, k, part, chain_sem.at[k, part, way], (group, r, c + 2 * way - 1))

    def cross_copy(source, k, part, way):
        target = sibling if way == 0 else across
        return transfer(source, COL + k, part, cross_sem.at[k, part, way], (group, target, c))

    def chain_sends(k, part, finish):
        for way in range(2):
            fits = jnp.logical_and(k >= c, c > 0) if way == 0 else jnp.logical_and(k <= c, c < COL - 1)

            @pl.when(fits)
            def _():
                copy = chain_copy(k, part, way)
                copy.wait_send() if finish else copy.start()

    def source_sends(k, part, finish):
        @pl.when(is_source)
        def _():
            for way in (1, 0):
                copy = cross_copy(k, k, part, way)
                copy.wait_send() if finish else copy.start()

    def relay_sends(k, part, finish):
        @pl.when(relays)
        def _():
            copy = cross_copy(COL + k, k, part, 0)
            copy.wait_send() if finish else copy.start()

    def normalise(values, gain_ref, bias_ref):
        center = jnp.mean(values, axis=-1, keepdims=True)
        moved = values - center
        spread = jnp.mean(jnp.square(moved), axis=-1, keepdims=True)
        return moved * lax.rsqrt(spread + 1e-05) * gain_ref[...] + bias_ref[...]

    loads = [
        pltpu.make_async_copy(source, target, load_sem.at[index])
        for index, (source, target) in enumerate((
            (pair_hbm, pair_ref), (in_gain_hbm, in_gain_ref), (in_bias_hbm, in_bias_ref),
            (w_gate_hbm, w_gate_ref), (w_left_hbm, w_left_ref), (lengths_hbm, lengths_ref),
            (w_right_hbm, w_right_ref), (mid_gain_hbm, mid_gain_ref),
            (mid_bias_hbm, mid_bias_ref), (w_out_hbm, w_out_ref),
        ))
    ]
    for load in loads:
        load.start()
    barrier = pltpu.get_barrier_semaphore()
    for step in range(1, ROW):
        pl.semaphore_signal(
            barrier, inc=1, device_id=(group, (r + step) % ROW, c), device_id_type=MESH
        )

    @pl.when(c > 0)
    def _():
        pl.semaphore_signal(barrier, inc=1, device_id=(group, r, c - 1), device_id_type=MESH)

    @pl.when(c < COL - 1)
    def _():
        pl.semaphore_signal(barrier, inc=1, device_id=(group, r, c + 1), device_id_type=MESH)

    def norm_piece(part):
        rows = rows_of(part)
        values = pair_ref[rows, :].astype(jnp.float32)
        held[c, rows, :] = normalise(values, in_gain_ref, in_bias_ref).astype(jnp.bfloat16)

    for load in loads[:3]:
        load.wait()
    norm_piece(0)
    pl.semaphore_wait(
        barrier, ROW - 1 + jnp.where(c > 0, 1, 0) + jnp.where(c < COL - 1, 1, 0)
    )
    for part in range(CHUNKS):
        if part > 0:
            norm_piece(part)
        chain_sends(c, part, False)
        source_sends(c, part, False)

    for load in loads[3:]:
        load.wait()

    def piece_rows(t):
        return pl.ds(pl.multiple_of(t * piece, 16), piece)

    def own_piece(t, carry):
        rows = piece_rows(t)
        gate[rows, :] = half_gate(
            jnp.dot(held[c, rows, :], w_gate_ref[...], preferred_element_type=jnp.float32)
        )
        triangle[rows, :] = jnp.zeros((piece, width), jnp.float32)
        return carry

    lax.fori_loop(0, pieces, own_piece, 0)

    def edge(slot, weight_ref, rows):
        projected = jnp.dot(
            held[slot, rows, :], weight_ref[...], preferred_element_type=jnp.float32
        )
        return projected[:, :width] * half_gate(projected[:, width:])

    def left_part(k):
        def left_piece(t, carry):
            rows = piece_rows(t)
            left_edge[rows, :] = edge(k, w_left_ref, rows)
            return carry

        lax.fori_loop(0, pieces, left_piece, 0)

    def right_part(k):
        slot = jnp.where(is_source, k, COL + k)
        mask_k = present(k * side, (side, width))

        def right_piece(t, carry):
            rows = piece_rows(t)
            value = edge(slot, w_right_ref, rows).reshape(PIECE, side, width) * mask_k[None]
            right_edge[rows, :] = value.reshape(piece, width)
            return carry

        lax.fori_loop(0, pieces, right_piece, 0)

    def multiply():
        def some_rows(block, carry):
            base = pl.multiple_of(block * (8 * side), 8)

            def add_k(k, sums):
                rights = [
                    right_edge[pl.ds(tile * 8 * side + k, 8, stride=side), :]
                    for tile in range(tiles)
                ]
                new = []
                for i in range(8):
                    left = left_edge[pl.ds(base + i * side + k, 1), :]
                    for tile in range(tiles):
                        new.append(sums[i * tiles + tile] + left * rights[tile])
                return tuple(new)

            where = [
                pl.ds(pl.multiple_of(base + i * side + tile * 8, 8), 8)
                for i in range(8)
                for tile in range(tiles)
            ]
            sums = tuple(triangle[rows, :] for rows in where)
            sums = lax.fori_loop(0, side, add_k, sums, unroll=8)
            for rows, value in zip(where, sums):
                triangle[rows, :] = value
            return carry

        lax.fori_loop(0, side // 8, some_rows, 0)

    def at_distance(distance, act):
        def on_side(sign, carry):
            k = c + (2 * sign - 1) * distance
            inside = jnp.logical_and(k >= 0, k < COL)

            @pl.when(jnp.logical_and(inside, jnp.logical_or(distance > 0, sign > 0)))
            def _():
                act(k)

            return carry

        lax.fori_loop(0, 2, on_side, 0)

    def gather(distance):
        def pass_on(part, carry):
            def act(k):
                chain_copy(k, part, 0).wait_recv()
                chain_sends(k, part, False)
                source_sends(k, part, False)

            at_distance(distance, act)
            return carry

        lax.fori_loop(0, CHUNKS, pass_on, 0)

    def receive_right(k):
        @pl.when(jnp.logical_not(is_source))
        def _():
            def pass_on(part, carry):
                cross_copy(k, k, part, 0).wait_recv()
                relay_sends(k, part, False)
                return carry

            lax.fori_loop(0, CHUNKS, pass_on, 0)

    def work(k):
        left_part(k)
        receive_right(k)
        right_part(k)
        multiply()

    def stage(distance, carry):
        @pl.when(distance < COL)
        def _():
            gather(distance)

        at_distance(distance - 1, work)
        return carry

    lax.fori_loop(1, COL + 1, stage, 0)

    mask_j = present(c * side, (side, width))

    def finish_piece(t, carry):
        rows = piece_rows(t)
        parts = []
        for i in range(PIECE):
            mask_i = present(r * side + t * PIECE + i, (1, width))
            parts.append(mask_i * mask_j)
        mask = jnp.concatenate(parts, axis=0)
        normed = normalise(triangle[rows, :] * mask, mid_gain_ref, mid_bias_ref)
        projected = jnp.dot(
            normed.astype(jnp.bfloat16), w_out_ref[...], preferred_element_type=jnp.float32
        )
        out_ref[rows, :] = (gate[rows, :] * projected).astype(out_ref.dtype)
        return carry

    lax.fori_loop(0, pieces, finish_piece, 0)

    def drain(index, carry):
        k, part = index // CHUNKS, index % CHUNKS
        chain_sends(k, part, True)
        source_sends(k, part, True)
        relay_sends(k, part, True)
        return carry

    lax.fori_loop(0, COL * CHUNKS, drain, 0)


def fused_shards(pair_act, lengths, in_gain, in_bias, w_left, w_right, w_gate, mid_gain, mid_bias, w_out):
    side, _, width = pair_act.shape
    positions = side * side
    slot_len = side * ROW // lengths.shape[0]
    vmem = pl.BlockSpec(memory_space=pltpu.VMEM)
    out = pl.pallas_call(
        functools.partial(fused_kernel, side=side, slot_len=slot_len),
        out_shape=jax.ShapeDtypeStruct((positions, width), jnp.bfloat16),
        in_specs=[pl.BlockSpec(memory_space=pltpu.HBM)] * 10,
        out_specs=vmem,
        scratch_shapes=[
            pltpu.SMEM(lengths.shape, jnp.int32),
            pltpu.VMEM((positions, width), jnp.bfloat16),
            pltpu.VMEM((1, width), jnp.float32),
            pltpu.VMEM((1, width), jnp.float32),
            pltpu.VMEM(w_left.shape, jnp.bfloat16),
            pltpu.VMEM(w_right.shape, jnp.bfloat16),
            pltpu.VMEM(w_gate.shape, jnp.bfloat16),
            pltpu.VMEM((1, width), jnp.float32),
            pltpu.VMEM((1, width), jnp.float32),
            pltpu.VMEM(w_out.shape, jnp.bfloat16),
            pltpu.SemaphoreType.DMA((10,)),
            pltpu.VMEM((2 * COL, positions, width), jnp.bfloat16),
            pltpu.VMEM((positions, width), jnp.float32),
            pltpu.VMEM((positions, width), jnp.float32),
            pltpu.VMEM((positions, width), jnp.float32),
            pltpu.VMEM((positions, width), jnp.float32),
            pltpu.SemaphoreType.DMA((2 * COL, CHUNKS)),
            pltpu.SemaphoreType.DMA((COL, CHUNKS, 2)),
            pltpu.SemaphoreType.DMA((COL, CHUNKS, 2)),
        ],
        compiler_params=pltpu.CompilerParams(
            collective_id=0, has_side_effects=True, vmem_limit_bytes=56 * 1024 * 1024
        ),
    )(
        lengths, pair_act.reshape(positions, width), in_gain[None], in_bias[None], w_left, w_right,
        w_gate, mid_gain[None], mid_bias[None], w_out,
    )
    return out.reshape(side, side, width)


def solution(mesh):
    in_specs = (
        P(("groups", "row"), "col", None),
        P("groups"),
        P(),
        P(),
        P(),
        P(),
        P(),
        P(),
        P(),
        P(),
    )
    out_specs = P(("groups", "row"), "col", None)
    shards = plain_shards
    if mesh.shape["row"] == 4 and mesh.shape["col"] == 4:
        shards = fused_shards
    return jax.shard_map(shards, mesh=mesh, in_specs=in_specs, out_specs=out_specs, check_vma=False)
```

```python
import functools

import jax
import jax.numpy as jnp
from jax import lax
from jax.experimental import pallas as pl
from jax.experimental.pallas import tpu as pltpu
from jax.sharding import PartitionSpec as P


def layer_norm(values, gain, bias):
    center = jnp.mean(values, axis=-1, keepdims=True)
    spread = jnp.mean(jnp.square(values - center), axis=-1, keepdims=True)
    return (values - center) / jnp.sqrt(spread + 1e-05) * gain + bias


def in_crop(residue_ids, lengths, slot_len):
    chain_of = residue_ids // slot_len
    chosen = chain_of[:, None] == jnp.arange(lengths.shape[0], dtype=jnp.int32)[None, :]
    chain_len = jnp.sum(jnp.where(chosen, lengths[None, :], 0), axis=1)
    return (residue_ids % slot_len < chain_len).astype(jnp.float32)


def plain_shards(pair_act, lengths, in_gain, in_bias, w_left, w_right, w_gate, mid_gain, mid_bias, w_out):
    rows_here, cols_here, width = pair_act.shape
    hidden = w_out.shape[0]
    residues = rows_here * lax.axis_size("row")
    slot_len = residues // lengths.shape[0]
    row_ids = lax.axis_index("row") * rows_here + jnp.arange(rows_here, dtype=jnp.int32)
    col_ids = lax.axis_index("col") * cols_here + jnp.arange(cols_here, dtype=jnp.int32)
    pair_mask = (
        in_crop(row_ids, lengths, slot_len)[:, None] * in_crop(col_ids, lengths, slot_len)[None, :]
    )
    pair_norm = layer_norm(pair_act.astype(jnp.float32), in_gain, in_bias).astype(jnp.bfloat16)
    pair_norm = pair_norm.reshape(rows_here * cols_here, width)

    def edge_panel(weight):
        projected = jnp.dot(pair_norm, weight, preferred_element_type=jnp.float32)
        projected = projected.reshape(rows_here, cols_here, 2 * hidden)
        gated = (
            pair_mask[:, :, None]
            * jax.nn.sigmoid(projected[:, :, hidden:])
            * projected[:, :, :hidden]
        )
        return jnp.transpose(gated.astype(jnp.bfloat16), (2, 0, 1))

    left_edge = edge_panel(w_left)
    right_edge = edge_panel(w_right)
    partial_value = jnp.einsum(
        "hik,hjk->hij",
        left_edge,
        lax.all_gather(right_edge, "row", axis=1, tiled=True),
        preferred_element_type=jnp.float32,
    )
    triangle = lax.psum_scatter(partial_value, "col", scatter_dimension=2, tiled=True)
    triangle = jnp.transpose(triangle, (1, 2, 0))
    normed = layer_norm(triangle, mid_gain, mid_bias).astype(jnp.bfloat16)
    out_gate = jax.nn.sigmoid(jnp.dot(pair_norm, w_gate, preferred_element_type=jnp.float32))
    projected_out = jnp.dot(
        normed.reshape(rows_here * cols_here, hidden), w_out, preferred_element_type=jnp.float32
    )
    return (out_gate * projected_out).reshape(rows_here, cols_here, width).astype(jnp.bfloat16)


MESH = pl.DeviceIdType.MESH
ROW, COL = 4, 4
CHUNKS = 5
PIECE = 40


def half_gate(values):
    return 0.5 * jnp.tanh(0.5 * values) + 0.5


def fused_kernel(
    lengths_hbm, pair_hbm, in_gain_hbm, in_bias_hbm, w_left_hbm, w_right_hbm, w_gate_hbm,
    mid_gain_hbm, mid_bias_hbm, w_out_hbm, out_ref,
    lengths_ref, pair_ref, in_gain_ref, in_bias_ref, w_left_ref, w_right_ref, w_gate_ref,
    mid_gain_ref, mid_bias_ref, w_out_ref, load_sem, held, left_edge, right_edge, triangle, gate, got_sem, chain_sem, cross_sem,
    *, side, slot_len,
):
    group, r, c = lax.axis_index("groups"), lax.axis_index("row"), lax.axis_index("col")
    positions, width = pair_ref.shape
    chunk = positions // CHUNKS
    piece = PIECE * side
    pieces = positions // piece
    tiles = side // 8
    chains = lengths_ref.shape[0]
    is_source = r == c
    same_core = r % 2 == c % 2
    same_chip = r // 2 == c // 2
    relays = jnp.logical_and(same_core, jnp.logical_not(same_chip))
    sibling = r + 1 - 2 * (r % 2)
    across = (r + 2) % ROW

    def present(first, extent):
        ids = first + lax.broadcasted_iota(jnp.int32, extent, len(extent) - 2)
        chosen = jnp.zeros(extent, jnp.float32)
        for chain in range(chains):
            start = chain * slot_len
            inside = jnp.logical_and(ids >= start, ids < start + lengths_ref[chain])
            inside = jnp.logical_and(inside, ids < start + slot_len)
            chosen = chosen + jnp.where(inside, 1.0, 0.0)
        return chosen

    def rows_of(part):
        return pl.ds(pl.multiple_of(part * chunk, 16), chunk)

    def transfer(source, target, part, send, device):
        return pltpu.make_async_remote_copy(
            src_ref=held.at[source, rows_of(part), :],
            dst_ref=held.at[target, rows_of(part), :],
            send_sem=send,
            recv_sem=got_sem.at[target, part],
            device_id=device,
            device_id_type=MESH,
        )

    def chain_copy(k, part, way):
        return transfer(k, k, part, chain_sem.at[k, part, way], (group, r, c + 2 * way - 1))

    def cross_copy(source, k, part, way):
        target = sibling if way == 0 else across
        return transfer(source, COL + k, part, cross_sem.at[k, part, way], (group, target, c))

    def chain_sends(k, part, finish):
        for way in range(2):
            fits = jnp.logical_and(k >= c, c > 0) if way == 0 else jnp.logical_and(k <= c, c < COL - 1)

            @pl.when(fits)
            def _():
                copy = chain_copy(k, part, way)
                copy.wait_send() if finish else copy.start()

    def source_sends(k, part, finish):
        @pl.when(is_source)
        def _():
            for way in (1, 0):
                copy = cross_copy(k, k, part, way)
                copy.wait_send() if finish else copy.start()

    def relay_sends(k, part, finish):
        @pl.when(relays)
        def _():
            copy = cross_copy(COL + k, k, part, 0)
            copy.wait_send() if finish else copy.start()

    def normalise(values, gain_ref, bias_ref):
        center = jnp.mean(values, axis=-1, keepdims=True)
        moved = values - center
        spread = jnp.mean(jnp.square(moved), axis=-1, keepdims=True)
        return moved * lax.rsqrt(spread + 1e-05) * gain_ref[...] + bias_ref[...]

    loads = [
        pltpu.make_async_copy(source, target, load_sem.at[index])
        for index, (source, target) in enumerate((
            (pair_hbm, pair_ref), (in_gain_hbm, in_gain_ref), (in_bias_hbm, in_bias_ref),
            (w_gate_hbm, w_gate_ref), (w_left_hbm, w_left_ref), (lengths_hbm, lengths_ref),
            (w_right_hbm, w_right_ref), (mid_gain_hbm, mid_gain_ref),
            (mid_bias_hbm, mid_bias_ref), (w_out_hbm, w_out_ref),
        ))
    ]
    for load in loads:
        load.start()
    barrier = pltpu.get_barrier_semaphore()
    for step in range(1, ROW):
        pl.semaphore_signal(
            barrier, inc=1, device_id=(group, (r + step) % ROW, c), device_id_type=MESH
        )

    @pl.when(c > 0)
    def _():
        pl.semaphore_signal(barrier, inc=1, device_id=(group, r, c - 1), device_id_type=MESH)

    @pl.when(c < COL - 1)
    def _():
        pl.semaphore_signal(barrier, inc=1, device_id=(group, r, c + 1), device_id_type=MESH)

    def norm_piece(part):
        rows = rows_of(part)
        values = pair_ref[rows, :].astype(jnp.float32)
        held[c, rows, :] = normalise(values, in_gain_ref, in_bias_ref).astype(jnp.bfloat16)

    for load in loads[:3]:
        load.wait()
    norm_piece(0)
    pl.semaphore_wait(
        barrier, ROW - 1 + jnp.where(c > 0, 1, 0) + jnp.where(c < COL - 1, 1, 0)
    )
    for part in range(CHUNKS):
        if part > 0:
            norm_piece(part)
        chain_sends(c, part, False)
        source_sends(c, part, False)

    for load in loads[3:]:
        load.wait()

    def piece_rows(t):
        return pl.ds(pl.multiple_of(t * piece, 16), piece)

    def own_piece(t, carry):
        rows = piece_rows(t)
        gate[rows, :] = half_gate(
            jnp.dot(held[c, rows, :], w_gate_ref[...], preferred_element_type=jnp.float32)
        )
        triangle[rows, :] = jnp.zeros((piece, width), jnp.float32)
        return carry

    lax.fori_loop(0, pieces, own_piece, 0)

    def edge(slot, weight_ref, rows):
        projected = jnp.dot(
            held[slot, rows, :], weight_ref[...], preferred_element_type=jnp.float32
        )
        return projected[:, :width] * half_gate(projected[:, width:])

    def left_part(k):
        def left_piece(t, carry):
            rows = piece_rows(t)
            left_edge[rows, :] = edge(k, w_left_ref, rows)
            return carry

        lax.fori_loop(0, pieces, left_piece, 0)

    tile_rows = positions // tiles

    def right_tile(k, tile):
        slot = jnp.where(is_source, k, COL + k)
        mask_k = present(k * side, (side, width))
        rows = pl.ds(pl.multiple_of(tile * tile_rows, 16), tile_rows)
        value = edge(slot, w_right_ref, rows).reshape(8, side, width) * mask_k[None]
        right_edge[...] = value.reshape(tile_rows, width)

        def add_k(k, sums):
            right = right_edge[pl.ds(k, 8, stride=side), :]
            return tuple(
                total + left_edge[pl.ds(i * side + k, 1), :] * right
                for i, total in enumerate(sums)
            )

        where = [
            pl.ds(pl.multiple_of(i * side + tile * 8, 8), 8) for i in range(side)
        ]
        sums = tuple(triangle[rows, :] for rows in where)
        sums = lax.fori_loop(0, side, add_k, sums, unroll=8)
        for rows, value in zip(where, sums):
            triangle[rows, :] = value

    def at_distance(distance, act):
        def on_side(sign, carry):
            k = c + (2 * sign - 1) * distance
            inside = jnp.logical_and(k >= 0, k < COL)

            @pl.when(jnp.logical_and(inside, jnp.logical_or(distance > 0, sign > 0)))
            def _():
                act(k)

            return carry

        lax.fori_loop(0, 2, on_side, 0)

    def gather(distance):
        def pass_on(part, carry):
            def act(k):
                chain_copy(k, part, 0).wait_recv()
                chain_sends(k, part, False)
                source_sends(k, part, False)

            at_distance(distance, act)
            return carry

        lax.fori_loop(0, CHUNKS, pass_on, 0)

    def work(k):
        left_part(k)

        def each_tile(part, carry):
            @pl.when(jnp.logical_not(is_source))
            def _():
                cross_copy(k, k, part, 0).wait_recv()
                relay_sends(k, part, False)

            right_tile(k, part)
            return carry

        lax.fori_loop(0, CHUNKS, each_tile, 0)

    at_end = jnp.logical_or(c == 0, c == COL - 1)

    def stage(distance, carry):
        early = jnp.where(distance < 2, distance + 1, 0)
        late = jnp.where(distance == 0, 1, jnp.where(distance == 1, 0, distance))
        next_gather = jnp.where(at_end, late, early)

        @pl.when(next_gather > 0)
        def _():
            gather(next_gather)

        at_distance(distance, work)
        return carry

    lax.fori_loop(0, COL, stage, 0)

    mask_j = present(c * side, (side, width))

    def finish_piece(t, carry):
        rows = piece_rows(t)
        parts = []
        for i in range(PIECE):
            mask_i = present(r * side + t * PIECE + i, (1, width))
            parts.append(mask_i * mask_j)
        mask = jnp.concatenate(parts, axis=0)
        normed = normalise(triangle[rows, :] * mask, mid_gain_ref, mid_bias_ref)
        projected = jnp.dot(
            normed.astype(jnp.bfloat16), w_out_ref[...], preferred_element_type=jnp.float32
        )
        out_ref[rows, :] = (gate[rows, :] * projected).astype(out_ref.dtype)
        return carry

    lax.fori_loop(0, pieces, finish_piece, 0)

    def drain(index, carry):
        k, part = index // CHUNKS, index % CHUNKS
        chain_sends(k, part, True)
        source_sends(k, part, True)
        relay_sends(k, part, True)
        return carry

    lax.fori_loop(0, COL * CHUNKS, drain, 0)


def fused_shards(pair_act, lengths, in_gain, in_bias, w_left, w_right, w_gate, mid_gain, mid_bias, w_out):
    side, _, width = pair_act.shape
    positions = side * side
    slot_len = side * ROW // lengths.shape[0]
    vmem = pl.BlockSpec(memory_space=pltpu.VMEM)
    out = pl.pallas_call(
        functools.partial(fused_kernel, side=side, slot_len=slot_len),
        out_shape=jax.ShapeDtypeStruct((positions, width), jnp.bfloat16),
        in_specs=[pl.BlockSpec(memory_space=pltpu.HBM)] * 10,
        out_specs=vmem,
        scratch_shapes=[
            pltpu.SMEM(lengths.shape, jnp.int32),
            pltpu.VMEM((positions, width), jnp.bfloat16),
            pltpu.VMEM((1, width), jnp.float32),
            pltpu.VMEM((1, width), jnp.float32),
            pltpu.VMEM(w_left.shape, jnp.bfloat16),
            pltpu.VMEM(w_right.shape, jnp.bfloat16),
            pltpu.VMEM(w_gate.shape, jnp.bfloat16),
            pltpu.VMEM((1, width), jnp.float32),
            pltpu.VMEM((1, width), jnp.float32),
            pltpu.VMEM(w_out.shape, jnp.bfloat16),
            pltpu.SemaphoreType.DMA((10,)),
            pltpu.VMEM((2 * COL, positions, width), jnp.bfloat16),
            pltpu.VMEM((positions, width), jnp.float32),
            pltpu.VMEM((8 * side, width), jnp.float32),
            pltpu.VMEM((positions, width), jnp.float32),
            pltpu.VMEM((positions, width), jnp.float32),
            pltpu.SemaphoreType.DMA((2 * COL, CHUNKS)),
            pltpu.SemaphoreType.DMA((COL, CHUNKS, 2)),
            pltpu.SemaphoreType.DMA((COL, CHUNKS, 2)),
        ],
        compiler_params=pltpu.CompilerParams(
            collective_id=0, has_side_effects=True, vmem_limit_bytes=56 * 1024 * 1024
        ),
    )(
        lengths, pair_act.reshape(positions, width), in_gain[None], in_bias[None], w_left, w_right,
        w_gate, mid_gain[None], mid_bias[None], w_out,
    )
    return out.reshape(side, side, width)


def solution(mesh):
    in_specs = (
        P(("groups", "row"), "col", None),
        P("groups"),
        P(),
        P(),
        P(),
        P(),
        P(),
        P(),
        P(),
        P(),
    )
    out_specs = P(("groups", "row"), "col", None)
    shards = plain_shards
    if mesh.shape["row"] == 4 and mesh.shape["col"] == 4:
        shards = fused_shards
    return jax.shard_map(shards, mesh=mesh, in_specs=in_specs, out_specs=out_specs, check_vma=False)
```

```python
import functools

import jax
import jax.numpy as jnp
from jax import lax
from jax.experimental import pallas as pl
from jax.experimental.pallas import tpu as pltpu
from jax.sharding import PartitionSpec as P


def layer_norm(values, gain, bias):
    center = jnp.mean(values, axis=-1, keepdims=True)
    spread = jnp.mean(jnp.square(values - center), axis=-1, keepdims=True)
    return (values - center) / jnp.sqrt(spread + 1e-05) * gain + bias


def in_crop(residue_ids, lengths, slot_len):
    chain_of = residue_ids // slot_len
    chosen = chain_of[:, None] == jnp.arange(lengths.shape[0], dtype=jnp.int32)[None, :]
    chain_len = jnp.sum(jnp.where(chosen, lengths[None, :], 0), axis=1)
    return (residue_ids % slot_len < chain_len).astype(jnp.float32)


def plain_shards(pair_act, lengths, in_gain, in_bias, w_left, w_right, w_gate, mid_gain, mid_bias, w_out):
    rows_here, cols_here, width = pair_act.shape
    hidden = w_out.shape[0]
    residues = rows_here * lax.axis_size("row")
    slot_len = residues // lengths.shape[0]
    row_ids = lax.axis_index("row") * rows_here + jnp.arange(rows_here, dtype=jnp.int32)
    col_ids = lax.axis_index("col") * cols_here + jnp.arange(cols_here, dtype=jnp.int32)
    pair_mask = (
        in_crop(row_ids, lengths, slot_len)[:, None] * in_crop(col_ids, lengths, slot_len)[None, :]
    )
    pair_norm = layer_norm(pair_act.astype(jnp.float32), in_gain, in_bias).astype(jnp.bfloat16)
    pair_norm = pair_norm.reshape(rows_here * cols_here, width)

    def edge_panel(weight):
        projected = jnp.dot(pair_norm, weight, preferred_element_type=jnp.float32)
        projected = projected.reshape(rows_here, cols_here, 2 * hidden)
        gated = (
            pair_mask[:, :, None]
            * jax.nn.sigmoid(projected[:, :, hidden:])
            * projected[:, :, :hidden]
        )
        return jnp.transpose(gated.astype(jnp.bfloat16), (2, 0, 1))

    left_edge = edge_panel(w_left)
    right_edge = edge_panel(w_right)
    partial_value = jnp.einsum(
        "hik,hjk->hij",
        left_edge,
        lax.all_gather(right_edge, "row", axis=1, tiled=True),
        preferred_element_type=jnp.float32,
    )
    triangle = lax.psum_scatter(partial_value, "col", scatter_dimension=2, tiled=True)
    triangle = jnp.transpose(triangle, (1, 2, 0))
    normed = layer_norm(triangle, mid_gain, mid_bias).astype(jnp.bfloat16)
    out_gate = jax.nn.sigmoid(jnp.dot(pair_norm, w_gate, preferred_element_type=jnp.float32))
    projected_out = jnp.dot(
        normed.reshape(rows_here * cols_here, hidden), w_out, preferred_element_type=jnp.float32
    )
    return (out_gate * projected_out).reshape(rows_here, cols_here, width).astype(jnp.bfloat16)


MESH = pl.DeviceIdType.MESH
ROW, COL = 4, 4
CHUNKS = 5
PIECE = 40


def half_gate(values):
    return 0.5 * jnp.tanh(0.5 * values) + 0.5


def fused_kernel(
    lengths_hbm, pair_hbm, in_gain_hbm, in_bias_hbm, w_left_hbm, w_right_hbm, w_gate_hbm,
    mid_gain_hbm, mid_bias_hbm, w_out_hbm, out_ref,
    lengths_ref, pair_ref, in_gain_ref, in_bias_ref, w_left_ref, w_right_ref, w_gate_ref,
    mid_gain_ref, mid_bias_ref, w_out_ref, load_sem, pair_sem, held, left_edge, right_edge, triangle, gate, got_sem, chain_sem, cross_sem,
    *, side, slot_len,
):
    group, r, c = lax.axis_index("groups"), lax.axis_index("row"), lax.axis_index("col")
    positions, width = pair_ref.shape
    chunk = positions // CHUNKS
    piece = PIECE * side
    pieces = positions // piece
    tiles = side // 8
    chains = lengths_ref.shape[0]
    is_source = r == c
    same_core = r % 2 == c % 2
    same_chip = r // 2 == c // 2
    relays = jnp.logical_and(same_core, jnp.logical_not(same_chip))
    sibling = r + 1 - 2 * (r % 2)
    across = (r + 2) % ROW

    def present(first, extent):
        ids = first + lax.broadcasted_iota(jnp.int32, extent, len(extent) - 2)
        chosen = jnp.zeros(extent, jnp.float32)
        for chain in range(chains):
            start = chain * slot_len
            inside = jnp.logical_and(ids >= start, ids < start + lengths_ref[chain])
            inside = jnp.logical_and(inside, ids < start + slot_len)
            chosen = chosen + jnp.where(inside, 1.0, 0.0)
        return chosen

    def rows_of(part):
        return pl.ds(pl.multiple_of(part * chunk, 16), chunk)

    def transfer(source, target, part, send, device):
        return pltpu.make_async_remote_copy(
            src_ref=held.at[source, rows_of(part), :],
            dst_ref=held.at[target, rows_of(part), :],
            send_sem=send,
            recv_sem=got_sem.at[target, part],
            device_id=device,
            device_id_type=MESH,
        )

    def chain_copy(k, part, way):
        return transfer(k, k, part, chain_sem.at[k, part, way], (group, r, c + 2 * way - 1))

    def cross_copy(source, k, part, way):
        target = sibling if way == 0 else across
        return transfer(source, COL + k, part, cross_sem.at[k, part, way], (group, target, c))

    def chain_sends(k, part, finish):
        for way in range(2):
            fits = jnp.logical_and(k >= c, c > 0) if way == 0 else jnp.logical_and(k <= c, c < COL - 1)

            @pl.when(fits)
            def _():
                copy = chain_copy(k, part, way)
                copy.wait_send() if finish else copy.start()

    def source_sends(k, part, finish):
        @pl.when(is_source)
        def _():
            for way in (1, 0):
                copy = cross_copy(k, k, part, way)
                copy.wait_send() if finish else copy.start()

    def relay_sends(k, part, finish):
        @pl.when(relays)
        def _():
            copy = cross_copy(COL + k, k, part, 0)
            copy.wait_send() if finish else copy.start()

    def normalise(values, gain_ref, bias_ref):
        center = jnp.mean(values, axis=-1, keepdims=True)
        moved = values - center
        spread = jnp.mean(jnp.square(moved), axis=-1, keepdims=True)
        return moved * lax.rsqrt(spread + 1e-05) * gain_ref[...] + bias_ref[...]

    loads = [
        pltpu.make_async_copy(source, target, load_sem.at[index])
        for index, (source, target) in enumerate((
            (in_gain_hbm, in_gain_ref), (in_bias_hbm, in_bias_ref),
            (w_gate_hbm, w_gate_ref), (w_left_hbm, w_left_ref), (lengths_hbm, lengths_ref),
            (w_right_hbm, w_right_ref), (mid_gain_hbm, mid_gain_ref),
            (mid_bias_hbm, mid_bias_ref), (w_out_hbm, w_out_ref),
        ))
    ]
    pair_loads = [
        pltpu.make_async_copy(
            pair_hbm.at[rows_of(part), :], pair_ref.at[rows_of(part), :], pair_sem.at[part]
        )
        for part in range(CHUNKS)
    ]
    for load in loads[:2] + pair_loads + loads[2:]:
        load.start()
    barrier = pltpu.get_barrier_semaphore()
    for step in range(1, ROW):
        pl.semaphore_signal(
            barrier, inc=1, device_id=(group, (r + step) % ROW, c), device_id_type=MESH
        )

    @pl.when(c > 0)
    def _():
        pl.semaphore_signal(barrier, inc=1, device_id=(group, r, c - 1), device_id_type=MESH)

    @pl.when(c < COL - 1)
    def _():
        pl.semaphore_signal(barrier, inc=1, device_id=(group, r, c + 1), device_id_type=MESH)

    def norm_piece(part):
        rows = rows_of(part)
        values = pair_ref[rows, :].astype(jnp.float32)
        held[c, rows, :] = normalise(values, in_gain_ref, in_bias_ref).astype(jnp.bfloat16)

    for load in loads[:2]:
        load.wait()
    pair_loads[0].wait()
    norm_piece(0)
    pl.semaphore_wait(
        barrier, ROW - 1 + jnp.where(c > 0, 1, 0) + jnp.where(c < COL - 1, 1, 0)
    )
    for part in range(CHUNKS):
        if part > 0:
            pair_loads[part].wait()
            norm_piece(part)
        chain_sends(c, part, False)
        source_sends(c, part, False)

    for load in loads[2:]:
        load.wait()

    def piece_rows(t):
        return pl.ds(pl.multiple_of(t * piece, 16), piece)

    def own_piece(t, carry):
        rows = piece_rows(t)
        gate[rows, :] = half_gate(
            jnp.dot(held[c, rows, :], w_gate_ref[...], preferred_element_type=jnp.float32)
        )
        triangle[rows, :] = jnp.zeros((piece, width), jnp.float32)
        return carry

    lax.fori_loop(0, pieces, own_piece, 0)

    def edge(slot, weight_ref, rows):
        projected = jnp.dot(
            held[slot, rows, :], weight_ref[...], preferred_element_type=jnp.float32
        )
        return projected[:, :width] * half_gate(projected[:, width:])

    def left_part(k):
        def left_piece(t, carry):
            rows = piece_rows(t)
            left_edge[rows, :] = edge(k, w_left_ref, rows)
            return carry

        lax.fori_loop(0, pieces, left_piece, 0)

    tile_rows = positions // tiles

    def right_tile(k, tile):
        slot = jnp.where(is_source, k, COL + k)
        mask_k = present(k * side, (side, width))
        rows = pl.ds(pl.multiple_of(tile * tile_rows, 16), tile_rows)
        value = edge(slot, w_right_ref, rows).reshape(8, side, width) * mask_k[None]
        right_edge[...] = value.reshape(tile_rows, width)

        def add_k(k, sums):
            right = right_edge[pl.ds(k, 8, stride=side), :]
            return tuple(
                total + left_edge[pl.ds(i * side + k, 1), :] * right
                for i, total in enumerate(sums)
            )

        where = [
            pl.ds(pl.multiple_of(i * side + tile * 8, 8), 8) for i in range(side)
        ]
        sums = tuple(triangle[rows, :] for rows in where)
        sums = lax.fori_loop(0, side, add_k, sums, unroll=8)
        for rows, value in zip(where, sums):
            triangle[rows, :] = value

    def at_distance(distance, act):
        def on_side(sign, carry):
            k = c + (2 * sign - 1) * distance
            inside = jnp.logical_and(k >= 0, k < COL)

            @pl.when(jnp.logical_and(inside, jnp.logical_or(distance > 0, sign > 0)))
            def _():
                act(k)

            return carry

        lax.fori_loop(0, 2, on_side, 0)

    def gather(distance):
        def pass_on(part, carry):
            def act(k):
                chain_copy(k, part, 0).wait_recv()
                chain_sends(k, part, False)
                source_sends(k, part, False)

            at_distance(distance, act)
            return carry

        lax.fori_loop(0, CHUNKS, pass_on, 0)

    def work(k):
        left_part(k)

        def each_tile(part, carry):
            @pl.when(jnp.logical_not(is_source))
            def _():
                cross_copy(k, k, part, 0).wait_recv()
                relay_sends(k, part, False)

            right_tile(k, part)
            return carry

        lax.fori_loop(0, CHUNKS, each_tile, 0)

    at_end = jnp.logical_or(c == 0, c == COL - 1)

    def stage(distance, carry):
        early = jnp.where(distance < 2, distance + 1, 0)
        late = jnp.where(distance == 0, 1, jnp.where(distance == 1, 0, distance))
        next_gather = jnp.where(at_end, late, early)

        @pl.when(next_gather > 0)
        def _():
            gather(next_gather)

        at_distance(distance, work)
        return carry

    lax.fori_loop(0, COL, stage, 0)

    mask_j = present(c * side, (side, width))

    def finish_piece(t, carry):
        rows = piece_rows(t)
        parts = []
        for i in range(PIECE):
            mask_i = present(r * side + t * PIECE + i, (1, width))
            parts.append(mask_i * mask_j)
        mask = jnp.concatenate(parts, axis=0)
        normed = normalise(triangle[rows, :] * mask, mid_gain_ref, mid_bias_ref)
        projected = jnp.dot(
            normed.astype(jnp.bfloat16), w_out_ref[...], preferred_element_type=jnp.float32
        )
        out_ref[rows, :] = (gate[rows, :] * projected).astype(out_ref.dtype)
        return carry

    lax.fori_loop(0, pieces, finish_piece, 0)

    def drain(index, carry):
        k, part = index // CHUNKS, index % CHUNKS
        chain_sends(k, part, True)
        source_sends(k, part, True)
        relay_sends(k, part, True)
        return carry

    lax.fori_loop(0, COL * CHUNKS, drain, 0)


def fused_shards(pair_act, lengths, in_gain, in_bias, w_left, w_right, w_gate, mid_gain, mid_bias, w_out):
    side, _, width = pair_act.shape
    positions = side * side
    slot_len = side * ROW // lengths.shape[0]
    vmem = pl.BlockSpec(memory_space=pltpu.VMEM)
    out = pl.pallas_call(
        functools.partial(fused_kernel, side=side, slot_len=slot_len),
        out_shape=jax.ShapeDtypeStruct((positions, width), jnp.bfloat16),
        in_specs=[pl.BlockSpec(memory_space=pltpu.HBM)] * 10,
        out_specs=vmem,
        scratch_shapes=[
            pltpu.SMEM(lengths.shape, jnp.int32),
            pltpu.VMEM((positions, width), jnp.bfloat16),
            pltpu.VMEM((1, width), jnp.float32),
            pltpu.VMEM((1, width), jnp.float32),
            pltpu.VMEM(w_left.shape, jnp.bfloat16),
            pltpu.VMEM(w_right.shape, jnp.bfloat16),
            pltpu.VMEM(w_gate.shape, jnp.bfloat16),
            pltpu.VMEM((1, width), jnp.float32),
            pltpu.VMEM((1, width), jnp.float32),
            pltpu.VMEM(w_out.shape, jnp.bfloat16),
            pltpu.SemaphoreType.DMA((9,)),
            pltpu.SemaphoreType.DMA((CHUNKS,)),
            pltpu.VMEM((2 * COL, positions, width), jnp.bfloat16),
            pltpu.VMEM((positions, width), jnp.float32),
            pltpu.VMEM((8 * side, width), jnp.float32),
            pltpu.VMEM((positions, width), jnp.float32),
            pltpu.VMEM((positions, width), jnp.float32),
            pltpu.SemaphoreType.DMA((2 * COL, CHUNKS)),
            pltpu.SemaphoreType.DMA((COL, CHUNKS, 2)),
            pltpu.SemaphoreType.DMA((COL, CHUNKS, 2)),
        ],
        compiler_params=pltpu.CompilerParams(
            collective_id=0, has_side_effects=True, vmem_limit_bytes=56 * 1024 * 1024
        ),
    )(
        lengths, pair_act.reshape(positions, width), in_gain[None], in_bias[None], w_left, w_right,
        w_gate, mid_gain[None], mid_bias[None], w_out,
    )
    return out.reshape(side, side, width)


def solution(mesh):
    in_specs = (
        P(("groups", "row"), "col", None),
        P("groups"),
        P(),
        P(),
        P(),
        P(),
        P(),
        P(),
        P(),
        P(),
    )
    out_specs = P(("groups", "row"), "col", None)
    shards = plain_shards
    if mesh.shape["row"] == 4 and mesh.shape["col"] == 4:
        shards = fused_shards
    return jax.shard_map(shards, mesh=mesh, in_specs=in_specs, out_specs=out_specs, check_vma=False)
```
